32 devices in a mesh: chan: 8 (over z, y), row: 4 (over x, core).
Axes of the slice: x: 2, y: 2, z: 4, core: 2. Of those that a mesh axis runs over, the one named last changes fastest.
Arguments:
- eta_pp: float32 [8, 1024, 1024], P('chan', 'row'), as said below
- ham_pp: float32 [8, 1024, 1024], P('chan', 'row'), as said below
- block_size: int32 [8], P('chan'), may hold values from 128 to 1024, as said below
- pp_occupancy: float32 [8, 1024], P('chan'), may hold values from -1 to 1
- ph_occupancy: float32 [8, 1024], P('chan'), may hold values from -1 to 1
- coupling: float32 [8, 8, 128, 128], P('chan'), may hold values from -0.5 to 0.5
- channel_weight: float32 [8], P('chan'), may hold values from 0.02 to 1
- orbit_of: int32 [8, 1024], P('chan', 'row'), may hold values from 0 to 239
- tile_target: int32 [8, 4, 256], P('chan', 'row'), may hold values from 0 to 7, as said below
- tile_source: int32 [8, 4, 256], P('chan', 'row'), may hold values from 0 to 7, as said below
Outputs:
- comm: float32 [8, 1024, 1024], P('chan', 'row')
- onebody: float32 [240], replicated
The draws below stay inside these ranges and needn't reach their ends.
Inputs may be any that keep to these rules, and one draw needn't show every extreme that they name: Each block of eta_pp is antisymmetric: eta_pp[c, a, b] = -eta_pp[c, b, a]. Each block of ham_pp is symmetric: ham_pp[c, a, b] = ham_pp[c, b, a]. `block_size`: some channel has order 1024. Within each row group, at most 48 tiles of one block go to one block, and in every draw and row group every block sends exactly 48 tiles to some block. For every row group r and blocks c, p, the count of t with tile_target[c, r, t] = p equals the count of q with tile_source[p, r, q] = c. `tile_source`: agrees with tile_target as stated there.
All inputs are finite; a program needn't handle non-finite values.
Results may differ from the reference program's by a relative error of at most 0.000078.
Values sent between devices are 32-bit elements; how exact they have to be, the bound alone decides.
A program may use at most 64 MiB of HBM per device.

```python
import math
import jax
import jax.numpy as jnp
from jax import lax

BLK = 1024
TW = 128
TR = 8
NORB = 240
NCH = 8
NRB = 4
TQ = 256
CAP = 48


def route_tables(key):
    shift_key, left_key, right_key, place_key = jax.random.split(key, 4)
    pool_size = CAP * NCH
    base_value = jnp.arange(pool_size, dtype=jnp.int32) // CAP

    def one_group(group_key):
        order_key, pick_key = jax.random.split(group_key)
        scores = jax.random.permutation(order_key, pool_size).astype(jnp.int32)
        chosen = jax.random.randint(pick_key, (), 0, NCH, dtype=jnp.int32)
        scores = jnp.where(base_value == chosen, -1 - jnp.arange(pool_size, dtype=jnp.int32), scores)
        return base_value[jnp.argsort(scores)][:TQ]
    shifts = jax.vmap(one_group)(jax.random.split(shift_key, NRB))
    left_perm = jax.random.permutation(left_key, NCH).astype(jnp.int32)
    right_perm = jax.random.permutation(right_key, NCH).astype(jnp.int32)
    channels = jnp.arange(NCH, dtype=jnp.int32)
    targets = left_perm[(right_perm[channels][:, None, None] + shifts[None]) % NCH]
    left_inverse = jnp.argsort(left_perm).astype(jnp.int32)
    right_inverse = jnp.argsort(right_perm).astype(jnp.int32)
    anchors = right_inverse[(left_inverse[channels][:, None, None] - shifts[None]) % NCH]
    shuffle = jax.vmap(lambda sub_key: jax.random.permutation(sub_key, TQ))(jax.random.split(place_key, NCH * NRB))
    shuffle = shuffle.reshape(NCH, NRB, TQ).astype(jnp.int32)
    anchors = jnp.take_along_axis(anchors, shuffle, axis=2)
    return (targets.astype(jnp.int32), anchors.astype(jnp.int32))


def draw_tile_target(key, part):
    tables = route_tables(key)
    return tables[0]


def draw_tile_source(key, part):
    tables = route_tables(key)
    return tables[1]


def draw_block_size(key, part):
    key = jax.random.fold_in(key, 7)
    size_key, pick_key = jax.random.split(key)
    sizes = jax.random.randint(size_key, (NCH,), BLK // 8, BLK + 1, dtype=jnp.int32)
    chosen = jax.random.randint(pick_key, (), 0, NCH, dtype=jnp.int32)
    return jnp.where(jnp.arange(NCH, dtype=jnp.int32) == chosen, BLK, sizes).astype(jnp.int32)


def paired_values(key, sign_factor, overall):
    value_key, scale_key = jax.random.split(key)
    raw_values = jax.random.normal(value_key, (NCH, BLK, BLK), jnp.float32)
    spread = jnp.exp(jax.random.uniform(scale_key, (NCH, BLK), jnp.float32, -0.3, 0.3))
    raw_values = raw_values * spread[:, :, None] * spread[:, None, :]
    return (raw_values + sign_factor * jnp.swapaxes(raw_values, 1, 2)) * (overall * 0.5 ** 0.5)


def draw_eta_pp(key, part):
    key = jax.random.fold_in(key, 11)
    return paired_values(key, -1.0, 1.0)


def draw_ham_pp(key, part):
    key = jax.random.fold_in(key, 13)
    return paired_values(key, 1.0, BLK ** (-0.5))


def with_ends(array, own_key, low, high):
    extent = array.shape
    spot = [jax.random.randint(jax.random.fold_in(own_key, axis), (), 0, extent[axis]) for axis in range(len(extent))]
    array = array.at[tuple(spot)].set(low)
    longest = extent.index(max(extent))
    spot[longest] = (spot[longest] + 1) % extent[longest]
    return array.at[tuple(spot)].set(high)


def block_levels(key, dims, pieces, least, top_value):
    factor_of, own = 1.0, jax.random.fold_in(key, 6)
    for position, shards_of in pieces:
        steps = jnp.exp(jax.random.uniform(jax.random.fold_in(own, position), (shards_of,), jnp.float32, least / len(pieces), top_value / len(pieces)))
        factor_of = factor_of * jnp.repeat(steps, dims[position] // shards_of).reshape([-1 if axis == position else 1 for axis in range(len(dims))])
    return factor_of


def noise(own_key, extent, width, reach, cuts=(), kind=jnp.bfloat16):
    result = width * jax.random.normal(own_key, extent, jnp.float32)
    if cuts:
        result = result * block_levels(own_key, extent, cuts, -0.22, 0.18)
    return jnp.clip(result, -reach, reach).astype(kind)


def setup_inputs(seed: int = 0) -> dict:
    splits = jax.random.split(jax.random.key(seed), 11)
    return {
        "eta_pp": draw_eta_pp(jax.random.fold_in(splits[10], 71), 0),
        "ham_pp": draw_ham_pp(jax.random.fold_in(splits[10], 71), 0),
        "block_size": draw_block_size(jax.random.fold_in(splits[10], 71), 0),
        "pp_occupancy": jnp.clip(jax.random.uniform(splits[3], (NCH, BLK), jnp.float32, -1.0, 1.0) * block_levels(splits[3], (NCH, BLK), ((0, 8),), -0.4, 0.0), -1.0, 1.0),
        "ph_occupancy": jnp.clip(jax.random.uniform(splits[4], (NCH, BLK), jnp.float32, -1.0, 1.0) * block_levels(splits[4], (NCH, BLK), ((0, 8),), -0.4, 0.0), -1.0, 1.0),
        "coupling": noise(splits[5], (NCH, BLK // TW, TW, TW), TW ** -0.5, 0.5, ((0, 8),), jnp.float32),
        "channel_weight": jnp.clip(jnp.exp(math.log(1.0) - 3.912023 * jax.random.uniform(splits[6], (NCH,), jnp.float32) ** block_levels(splits[6], (NCH,), ((0, 8),), -0.2, 0.2)), 0.02, 1.0),
        "orbit_of": with_ends(jax.random.randint(splits[7], (NCH, BLK), 0, NORB), jax.random.fold_in(splits[7], 1), 0, NORB - 1).astype(jnp.int32),
        "tile_target": draw_tile_target(jax.random.fold_in(splits[10], 71), 0),
        "tile_source": draw_tile_source(jax.random.fold_in(splits[10], 71), 0),
    }


precise = lax.Precision.HIGHEST

def tiles_of(blocks):
    group_rows = BLK // NRB
    arranged = blocks.reshape(NCH, NRB, group_rows // TR, TR, BLK // TW, TW)
    arranged = arranged.transpose(0, 1, 2, 4, 3, 5)
    return arranged.reshape(NCH, NRB, TQ, TR, TW)

def blocks_of(tile_set):
    group_rows = BLK // NRB
    arranged = tile_set.reshape(NCH, NRB, group_rows // TR, BLK // TW, TR, TW)
    arranged = arranged.transpose(0, 1, 2, 4, 3, 5)
    return arranged.reshape(NCH, BLK, BLK)

def mix_bands(tile_set, coupling, pattern):
    arranged = tile_set.reshape(NCH, NRB, TQ // (BLK // TW), BLK // TW, TR, TW)
    mixed = jnp.einsum(pattern, arranged, coupling, precision=precise)
    return mixed.reshape(NCH, NRB, TQ, TR, TW)

def locate(mine, other):
    tile_index = jnp.arange(TQ, dtype=jnp.int32)
    same_peer = mine[:, :, :, None] == mine[:, :, None, :]
    earlier = tile_index[None, None, None, :] < tile_index[None, None, :, None]
    peer_rank = lax.optimization_barrier(jnp.sum((same_peer & earlier).astype(jnp.int32), axis=3))
    sorted_index = jnp.argsort(other * TQ + tile_index, axis=2).astype(jnp.int32)
    channels = jnp.arange(NCH, dtype=jnp.int32)
    below = lax.optimization_barrier(jnp.sum((other[:, :, :, None] < channels).astype(jnp.int32), axis=2))
    groups = jnp.arange(NRB, dtype=jnp.int32)[None, :, None]
    first_slot = below[mine, groups, channels[:, None, None]]
    return sorted_index[mine, groups, first_slot + peer_rank]

def reference(eta_pp, ham_pp, block_size, pp_occupancy, ph_occupancy, coupling, channel_weight, orbit_of, tile_target, tile_source):
    states = jnp.arange(BLK, dtype=jnp.int32)
    live = (states[None, :] < block_size[:, None]).astype(jnp.float32)
    eta_masked = eta_pp * live[:, :, None] * live[:, None, :]
    ham_masked = ham_pp * live[:, :, None] * live[:, None, :]
    groups = jnp.arange(NRB, dtype=jnp.int32)[None, :, None]
    tile_of_position = locate(tile_source, tile_target)
    position_of_tile = locate(tile_target, tile_source)
    forward = 'prgbij,pbjk->prgbik'
    backward = 'prgbij,pbkj->prgbik'
    ph_eta = blocks_of(mix_bands(tiles_of(eta_masked)[tile_source, groups, tile_of_position], coupling, forward))
    ph_ham = blocks_of(mix_bands(tiles_of(ham_masked)[tile_source, groups, tile_of_position], coupling, forward))

    def ph_product(inputs):
        left_block, right_block, occupancy = inputs
        return jnp.dot(left_block * occupancy[None, :], right_block, precision=precise, preferred_element_type=jnp.float32)
    product = lax.map(ph_product, (ph_eta, ph_ham, ph_occupancy))
    back = blocks_of(mix_bands(tiles_of(product), coupling, backward)[tile_target, groups, position_of_tile])

    def finish(inputs):
        left_block, right_block, weights, extra, live_row = inputs
        ladder = jnp.dot(left_block * weights[None, :], right_block, precision=precise, preferred_element_type=jnp.float32)
        summed = ladder + extra
        return (summed + summed.T) * live_row[:, None] * live_row[None, :]
    comm = lax.map(finish, (eta_masked, ham_masked, pp_occupancy, back, live))
    diagonal = jnp.diagonal(comm, axis1=1, axis2=2)
    terms = channel_weight[:, None] * diagonal
    onebody = jax.ops.segment_sum(terms.reshape(-1), orbit_of.reshape(-1), num_segments=NORB)
    return (comm, onebody * math.sqrt(NORB / (NCH * BLK)))
```

```python
import functools
import math

import jax
import jax.numpy as jnp
from jax import lax
from jax.experimental import pallas as pl
from jax.experimental.pallas import tpu as pltpu
from jax.sharding import PartitionSpec as P

TW = 128
TR = 8
NORB = 240
OPAD = 256
MESH = pl.DeviceIdType.MESH
F32 = jnp.float32
BF16 = jnp.bfloat16
ROW_DIMS = (((1,), (1,)), ((), ()))
COL_DIMS = (((1,), (0,)), ((), ()))


def group_rank(labels):
    length = labels.shape[-1]
    position = jnp.arange(length, dtype=jnp.int32)
    same_label = labels[:, :, None] == labels[:, None, :]
    before = position[None, :] < position[:, None]
    return jnp.sum((same_label & before).astype(jnp.int32), axis=-1)


def split(value):
    high = value.astype(BF16)
    return high, (value - high.astype(F32)).astype(BF16)


def dot3(left, right, dims=COL_DIMS):
    mul = functools.partial(lax.dot_general, dimension_numbers=dims, preferred_element_type=F32)
    return mul(left[0], right[0]) + (mul(left[0], right[1]) + mul(left[1], right[0]))


def kernel(
    n,
    cap,
    eta_ref,
    ham_ref,
    size_ref,
    pp_ref,
    ph_ref,
    coup_ref,
    weight_ref,
    orbit_ref,
    pack_ref,
    take_ref,
    back_pack_ref,
    back_take_ref,
    comm_ref,
    onebody_ref,
    ham_tiles,
    eta_tiles,
    ham_send,
    eta_send,
    ham_recv,
    eta_recv,
    full_ham,
    full_ph,
    mixed,
    left_hi,
    left_lo,
    lad_hi,
    lad_lo,
    total,
    back_send,
    back_recv,
    turned_send,
    turned_recv,
    row_sums,
    chan_sums,
    a2a_send,
    a2a_recv,
    gather_send,
    gather_recv,
    turn_send,
    turn_recv,
    rsum_send,
    rsum_recv,
    csum_send,
    csum_recv,
):
    me = lax.axis_index("chan")
    row = lax.axis_index("row")
    rows, cols = eta_ref.shape
    rgroups = cols // rows
    bands = cols // TW
    groups = rows // TR
    near = row + 1 - 2 * lax.rem(row, 2)
    far = lax.rem(row + 2, rgroups)
    diagonal_peer = lax.rem(near + 2, rgroups)
    half = n // 2

    def chan_peer(step):
        away = step // 2
        sign = 2 * lax.rem(step, 2) - 1
        return lax.rem(me + half + sign * away + n, n)

    barrier = pltpu.get_barrier_semaphore()

    @pl.loop(1, n)
    def _(step):
        pl.semaphore_signal(
            barrier, inc=1, device_id=(chan_peer(step), row), device_id_type=MESH
        )

    for other in range(1, rgroups):
        pl.semaphore_signal(
            barrier,
            inc=1,
            device_id=(me, lax.rem(row + other, rgroups)),
            device_id_type=MESH,
        )

    size = size_ref[0]
    row_ids = row * rows + lax.broadcasted_iota(jnp.int32, (rows, TW), 0)
    lane_ids = lax.broadcasted_iota(jnp.int32, (rows, TW), 1)

    def mask_of(band):
        return (row_ids < size) & (lane_ids + band * TW < size)

    for band in range(bands):
        lanes = slice(band * TW, (band + 1) * TW)
        value = jnp.where(mask_of(band), ham_ref[:, lanes], 0.0)
        full_ham[row, :, lanes] = value
        ham_tiles[band * groups : (band + 1) * groups] = value.reshape(groups, TR, TW)

    pl.semaphore_wait(barrier, n - 1 + rgroups - 1)

    def gather_copy(buf, phase, kind, slot, target):
        return pltpu.make_async_remote_copy(
            src_ref=buf.at[slot],
            dst_ref=buf.at[slot],
            send_sem=gather_send.at[phase, kind],
            recv_sem=gather_recv.at[phase, kind],
            device_id=(me, target),
            device_id_type=MESH,
        )

    def gather_start(buf, phase):
        gather_copy(buf, phase, 0, row, far).start()
        gather_copy(buf, phase, 1, row, near).start()

    def gather_forward(buf, phase):
        gather_copy(buf, phase, 0, far, far).wait_recv()
        gather_copy(buf, phase, 2, far, near).start()

    def gather_finish(buf, phase):
        gather_copy(buf, phase, 1, near, near).wait_recv()
        gather_copy(buf, phase, 2, diagonal_peer, near).wait_recv()

    def gather_drain(buf, phase):
        gather_copy(buf, phase, 0, row, far).wait_send()
        gather_copy(buf, phase, 1, row, near).wait_send()
        gather_copy(buf, phase, 2, far, near).wait_send()

    unit = next(u for u in (16, 12, 8, 6, 4, 3, 2, 1) if cap % u == 0)

    def pack_one(tiles, out, table, peer, base):
        @pl.loop(0, cap // unit)
        def _(part):
            for inner in range(unit):
                place = part * unit + inner
                out[base + place] = tiles[table[peer * cap + place]]

    def send_copy(send, recv, phase, peer, source):
        return pltpu.make_async_remote_copy(
            src_ref=send.at[pl.ds(peer * cap, cap)],
            dst_ref=recv.at[pl.ds(source * cap, cap)],
            send_sem=a2a_send.at[phase, peer],
            recv_sem=a2a_recv.at[phase, source],
            device_id=(peer, row),
            device_id_type=MESH,
        )

    def pack_send(tiles, send, recv, table, phase):
        @pl.loop(1, n)
        def _(step):
            peer = chan_peer(step)
            pack_one(tiles, send, table, peer, peer * cap)
            send_copy(send, recv, phase, peer, me).start()

        pack_one(tiles, recv, table, me, me * cap)

    def wait_sent(send, recv, phase):
        @pl.loop(1, n)
        def _(step):
            send_copy(send, recv, phase, chan_peer(step), me).wait_send()

    def wait_arrived(send, recv, phase):
        @pl.loop(1, n)
        def _(step):
            peer = chan_peer(step)
            send_copy(send, recv, phase, peer, peer).wait_recv()

    pack_send(ham_tiles, ham_send, ham_recv, pack_ref, 0)
    gather_start(full_ham, 0)

    for band in range(bands):
        lanes = slice(band * TW, (band + 1) * TW)
        value = jnp.where(mask_of(band), eta_ref[:, lanes], 0.0)
        eta_tiles[band * groups : (band + 1) * groups] = value.reshape(groups, TR, TW)
        high, low = split(value * pp_ref[:, lanes])
        lad_hi[:, lanes] = high
        lad_lo[:, lanes] = low

    wait_sent(ham_send, ham_recv, 0)
    pack_send(eta_tiles, eta_send, eta_recv, pack_ref, 1)

    def unpack(recv):
        @pl.loop(0, groups * bands // 16)
        def _(part):
            for inner in range(16):
                place = part * 16 + inner
                mixed[place] = recv[take_ref[place]]

    def mixed_band(band):
        tiles = mixed[band * groups : (band + 1) * groups].reshape(rows, TW)
        return dot3(split(tiles), split(coup_ref[band]))

    wait_arrived(ham_send, ham_recv, 0)
    unpack(ham_recv)
    for band in range(bands):
        full_ph[row, :, band * TW : (band + 1) * TW] = mixed_band(band)
    gather_start(full_ph, 1)
    gather_forward(full_ham, 0)
    gather_forward(full_ph, 1)

    wait_arrived(eta_send, eta_recv, 1)
    unpack(eta_recv)
    for band in range(bands):
        lanes = slice(band * TW, (band + 1) * TW)
        high, low = split(mixed_band(band) * ph_ref[:, lanes])
        left_hi[:, lanes] = high
        left_lo[:, lanes] = low
    gather_finish(full_ph, 1)

    def multiply(high_ref, low_ref, full):
        @pl.loop(0, cols // 256)
        def _(part):
            lanes = pl.ds(pl.multiple_of(part * 256, 256), 256)
            result = None
            for block in range(rgroups):
                depth = slice(block * rows, (block + 1) * rows)
                term = dot3(
                    (high_ref[:, depth], low_ref[:, depth]), split(full[block, :, lanes])
                )
                result = term if result is None else result + term
            total[:, lanes] = result

    multiply(left_hi, left_lo, full_ph)
    for band in range(bands):
        lanes = slice(band * TW, (band + 1) * TW)
        value = dot3(split(total[:, lanes]), split(coup_ref[band]), ROW_DIMS)
        mixed[band * groups : (band + 1) * groups] = value.reshape(groups, TR, TW)
    pack_send(mixed, back_send, back_recv, back_pack_ref, 2)

    gather_finish(full_ham, 0)
    multiply(lad_hi, lad_lo, full_ham)
    wait_sent(eta_send, eta_recv, 1)
    gather_drain(full_ham, 0)
    gather_drain(full_ph, 1)

    wait_arrived(back_send, back_recv, 2)

    @pl.loop(0, groups)
    def _(group):
        spot = pl.ds(pl.multiple_of(group * TR, TR), TR)
        for band in range(bands):
            lanes = slice(band * TW, (band + 1) * TW)
            total[spot, lanes] += back_recv[back_take_ref[group * bands + band]]

    def turn_copy(target, source):
        return pltpu.make_async_remote_copy(
            src_ref=turned_send.at[target],
            dst_ref=turned_recv.at[source],
            send_sem=turn_send.at[target],
            recv_sem=turn_recv.at[source],
            device_id=(me, target),
            device_id_type=MESH,
        )

    def block_of(target):
        return total[:, pl.ds(pl.multiple_of(target * rows, rows), rows)]

    for target in (far, diagonal_peer, near):
        turned_send[target] = block_of(target).T
        turn_copy(target, row).start()

    own = block_of(row)
    turned_recv[row] = own.T
    eye_rows = lax.broadcasted_iota(jnp.int32, (rows, rows), 0)
    eye_cols = lax.broadcasted_iota(jnp.int32, (rows, rows), 1)
    diagonal = jnp.sum(jnp.where(eye_rows == eye_cols, own, 0.0), axis=0, keepdims=True)
    alive = row * rows + lax.broadcasted_iota(jnp.int32, (1, rows), 1) < size
    terms = jnp.where(alive, (diagonal + diagonal) * weight_ref[0], 0.0)
    orbit_ids = lax.broadcasted_iota(jnp.int32, (OPAD, rows), 0)
    table = (orbit_ids == orbit_ref[...]).astype(F32)
    row_sums[row] = lax.dot_general(
        jnp.broadcast_to(terms, (TR, rows)),
        table,
        ROW_DIMS,
        precision=lax.Precision.HIGHEST,
        preferred_element_type=F32,
    )

    def rsum_copy(target, source):
        return pltpu.make_async_remote_copy(
            src_ref=row_sums.at[row],
            dst_ref=row_sums.at[source],
            send_sem=rsum_send.at[target],
            recv_sem=rsum_recv.at[source],
            device_id=(me, target),
            device_id_type=MESH,
        )

    for target in (far, diagonal_peer, near):
        rsum_copy(target, row).start()
    for target in (far, diagonal_peer, near):
        rsum_copy(target, target).wait_recv()
    partial_value = row_sums[0]
    for block in range(1, rgroups):
        partial_value = partial_value + row_sums[block]
    chan_sums[me] = partial_value

    def csum_copy(target, source):
        return pltpu.make_async_remote_copy(
            src_ref=chan_sums.at[me],
            dst_ref=chan_sums.at[source],
            send_sem=csum_send.at[target],
            recv_sem=csum_recv.at[source],
            device_id=(target, row),
            device_id_type=MESH,
        )

    @pl.loop(1, n)
    def _(step):
        csum_copy(chan_peer(step), me).start()

    for target in (near, far, diagonal_peer):
        turn_copy(target, target).wait_recv()
    for block in range(rgroups):
        for part in range(rows // TW):
            band = block * (rows // TW) + part
            lanes = slice(band * TW, (band + 1) * TW)
            value = total[:, lanes] + turned_recv[block, :, part * TW : (part + 1) * TW]
            comm_ref[:, lanes] = jnp.where(mask_of(band), value, 0.0)

    @pl.loop(1, n)
    def _(step):
        peer = chan_peer(step)
        csum_copy(peer, peer).wait_recv()

    onebody_ref[...] = lax.fori_loop(
        0, n, lambda i, acc: acc + chan_sums[i], jnp.zeros((TR, OPAD), F32)
    ) * math.sqrt(NORB / (n * cols))

    wait_sent(back_send, back_recv, 2)
    for target in (far, diagonal_peer, near):
        turn_copy(target, row).wait_send()
        rsum_copy(target, row).wait_send()

    @pl.loop(1, n)
    def _(step):
        csum_copy(chan_peer(step), me).wait_send()


def per_device(
    eta_pp,
    ham_pp,
    block_size,
    pp_occupancy,
    ph_occupancy,
    coupling,
    channel_weight,
    orbit_of,
    tile_target,
    tile_source,
):
    rows, cols = eta_pp.shape[1:]
    n = lax.axis_size("chan")
    rgroups = lax.axis_size("row")
    bands, groups = cols // TW, rows // TR
    count = bands * groups
    cap = max(2, 3 * count // (2 * n))
    slots = cap * n

    labels = jnp.stack([tile_target[0, 0], tile_source[0, 0]])
    slot_of = labels * cap + group_rank(labels)
    position = jnp.arange(count, dtype=jnp.int32)
    by_band = position % bands * groups + position // bands
    matches = slot_of[:, None, :] == jnp.arange(slots, dtype=jnp.int32)[None, :, None]
    pack = jnp.sum(jnp.where(matches, by_band, 0), axis=-1)
    take = slot_of[1].reshape(groups, bands).T.reshape(count)

    vmem = pl.BlockSpec(memory_space=pltpu.VMEM)
    smem = pl.BlockSpec(memory_space=pltpu.SMEM)
    dma = pltpu.SemaphoreType.DMA
    tile_buf = pltpu.VMEM((count, TR, TW), F32)
    slot_buf = pltpu.VMEM((slots, TR, TW), F32)
    full_buf = pltpu.VMEM((rgroups, rows, cols), F32)
    half_buf = pltpu.VMEM((rows, cols), BF16)
    comm, onebody = pl.pallas_call(
        functools.partial(kernel, n, cap),
        out_shape=(
            jax.ShapeDtypeStruct((rows, cols), F32),
            jax.ShapeDtypeStruct((TR, OPAD), F32),
        ),
        in_specs=[vmem, vmem, smem, vmem, vmem, vmem, smem, vmem, smem, smem, smem, smem],
        out_specs=(vmem, vmem),
        scratch_shapes=[
            tile_buf,
            tile_buf,
            slot_buf,
            slot_buf,
            slot_buf,
            slot_buf,
            full_buf,
            full_buf,
            tile_buf,
            half_buf,
            half_buf,
            half_buf,
            half_buf,
            pltpu.VMEM((rows, cols), F32),
            slot_buf,
            slot_buf,
            pltpu.VMEM((rgroups, rows, rows), F32),
            pltpu.VMEM((rgroups, rows, rows), F32),
            pltpu.VMEM((rgroups, TR, OPAD), F32),
            pltpu.VMEM((n, TR, OPAD), F32),
            dma((3, n)),
            dma((3, n)),
            dma((2, 3)),
            dma((2, 3)),
            dma((rgroups,)),
            dma((rgroups,)),
            dma((rgroups,)),
            dma((rgroups,)),
            dma((n,)),
            dma((n,)),
        ],
        compiler_params=pltpu.CompilerParams(
            collective_id=0, has_side_effects=True, vmem_limit_bytes=48 * 1024 * 1024
        ),
    )(
        eta_pp[0],
        ham_pp[0],
        block_size,
        pp_occupancy,
        ph_occupancy,
        coupling[0],
        channel_weight,
        orbit_of,
        pack[0],
        take,
        pack[1],
        slot_of[0],
    )
    return comm[None], onebody[0, :NORB]


def solution(mesh):
    return jax.shard_map(
        per_device,
        mesh=mesh,
        in_specs=(
            P("chan", "row", None),
            P("chan", "row", None),
            P("chan"),
            P("chan", None),
            P("chan", None),
            P("chan", None, None, None),
            P("chan"),
            P("chan", "row"),
            P("chan", "row", None),
            P("chan", "row", None),
        ),
        out_specs=(P("chan", "row", None), P()),
        check_vma=False,
    )
```

```python
import functools
import math

import jax
import jax.numpy as jnp
from jax import lax
from jax.experimental import pallas as pl
from jax.experimental.pallas import tpu as pltpu
from jax.sharding import PartitionSpec as P

TW = 128
TR = 8
NORB = 240
OPAD = 256
MESH = pl.DeviceIdType.MESH
F32 = jnp.float32
BF16 = jnp.bfloat16
ROW_DIMS = (((1,), (1,)), ((), ()))
COL_DIMS = (((1,), (0,)), ((), ()))


def group_rank(labels):
    length = labels.shape[-1]
    position = jnp.arange(length, dtype=jnp.int32)
    same_label = labels[:, :, None] == labels[:, None, :]
    before = position[None, :] < position[:, None]
    return jnp.sum((same_label & before).astype(jnp.int32), axis=-1)


def split(value):
    high = value.astype(BF16)
    return high, (value - high.astype(F32)).astype(BF16)


def dot3(left, right, dims=COL_DIMS):
    mul = functools.partial(lax.dot_general, dimension_numbers=dims, preferred_element_type=F32)
    return mul(left[0], right[0]) + (mul(left[0], right[1]) + mul(left[1], right[0]))


def kernel(
    n,
    cap,
    eta_hbm,
    ham_hbm,
    size_ref,
    pp_ref,
    ph_ref,
    coup_hbm,
    weight_ref,
    orbit_ref,
    pack_ref,
    take_ref,
    back_pack_ref,
    back_take_ref,
    comm_ref,
    onebody_ref,
    eta_ref,
    ham_ref,
    coup_ref,
    squares,
    ph_hi,
    ph_lo,
    ham_tiles,
    eta_tiles,
    ham_send,
    eta_send,
    ham_recv,
    eta_recv,
    full_ham,
    full_ph,
    mixed,
    left_hi,
    left_lo,
    lad_hi,
    lad_lo,
    total,
    back_send,
    back_recv,
    turned_send,
    turned_recv,
    row_sums,
    chan_sums,
    load_sem,
    a2a_send,
    a2a_recv,
    gather_send,
    gather_recv,
    turn_send,
    turn_recv,
    rsum_send,
    rsum_recv,
    csum_send,
    csum_recv,
):
    me = lax.axis_index("chan")
    row = lax.axis_index("row")
    rows, cols = eta_ref.shape
    rgroups = cols // rows
    bands = cols // TW
    groups = rows // TR
    near = row + 1 - 2 * lax.rem(row, 2)
    far = lax.rem(row + 2, rgroups)
    diagonal_peer = lax.rem(near + 2, rgroups)
    half = n // 2

    def chan_peer(step):
        away = step // 2
        sign = 2 * lax.rem(step, 2) - 1
        return lax.rem(me + half + sign * away + n, n)

    loads = [
        pltpu.make_async_copy(source, target, load_sem.at[place])
        for place, (source, target) in enumerate(
            ((ham_hbm, ham_ref), (eta_hbm, eta_ref), (coup_hbm, coup_ref))
        )
    ]
    for load in loads:
        load.start()

    barrier = pltpu.get_barrier_semaphore()

    @pl.loop(1, n)
    def _(step):
        pl.semaphore_signal(
            barrier, inc=1, device_id=(chan_peer(step), row), device_id_type=MESH
        )

    for other in range(1, rgroups):
        pl.semaphore_signal(
            barrier,
            inc=1,
            device_id=(me, lax.rem(row + other, rgroups)),
            device_id_type=MESH,
        )

    size = size_ref[0]
    row_ids = row * rows + lax.broadcasted_iota(jnp.int32, (rows, TW), 0)
    lane_ids = lax.broadcasted_iota(jnp.int32, (rows, TW), 1)

    def mask_of(band):
        return (row_ids < size) & (lane_ids + band * TW < size)

    loads[0].wait()
    for band in range(bands):
        lanes = slice(band * TW, (band + 1) * TW)
        value = jnp.where(mask_of(band), ham_ref[:, lanes], 0.0)
        full_ham[row, :, lanes] = value
        ham_tiles[band * groups : (band + 1) * groups] = value.reshape(groups, TR, TW)

    pl.semaphore_wait(barrier, n - 1 + rgroups - 1)

    def gather_copy(buf, phase, kind, slot, target):
        return pltpu.make_async_remote_copy(
            src_ref=buf.at[slot],
            dst_ref=buf.at[slot],
            send_sem=gather_send.at[phase, kind],
            recv_sem=gather_recv.at[phase, kind],
            device_id=(me, target),
            device_id_type=MESH,
        )

    def gather_start(buf, phase):
        gather_copy(buf, phase, 0, row, far).start()
        gather_copy(buf, phase, 1, row, near).start()

    def gather_forward(buf, phase):
        gather_copy(buf, phase, 0, far, far).wait_recv()
        gather_copy(buf, phase, 2, far, near).start()

    def gather_finish(buf, phase):
        gather_copy(buf, phase, 1, near, near).wait_recv()
        gather_copy(buf, phase, 2, diagonal_peer, near).wait_recv()

    def gather_drain(buf, phase):
        gather_copy(buf, phase, 0, row, far).wait_send()
        gather_copy(buf, phase, 1, row, near).wait_send()
        gather_copy(buf, phase, 2, far, near).wait_send()

    unit = next(u for u in (16, 12, 8, 6, 4, 3, 2, 1) if cap % u == 0)

    def pack_one(tiles, out, table, peer, base):
        @pl.loop(0, cap // unit)
        def _(part):
            for inner in range(unit):
                place = part * unit + inner
                out[base + place] = tiles[table[peer * cap + place]]

    def send_copy(send, recv, phase, peer, source):
        return pltpu.make_async_remote_copy(
            src_ref=send.at[pl.ds(peer * cap, cap)],
            dst_ref=recv.at[pl.ds(source * cap, cap)],
            send_sem=a2a_send.at[phase, peer],
            recv_sem=a2a_recv.at[phase, source],
            device_id=(peer, row),
            device_id_type=MESH,
        )

    def pack_send(tiles, send, recv, table, phase):
        @pl.loop(1, n)
        def _(step):
            peer = chan_peer(step)
            pack_one(tiles, send, table, peer, peer * cap)
            send_copy(send, recv, phase, peer, me).start()

        pack_one(tiles, recv, table, me, me * cap)

    def wait_sent(send, recv, phase):
        @pl.loop(1, n)
        def _(step):
            send_copy(send, recv, phase, chan_peer(step), me).wait_send()

    def wait_arrived(send, recv, phase):
        @pl.loop(1, n)
        def _(step):
            peer = chan_peer(step)
            send_copy(send, recv, phase, peer, peer).wait_recv()

    pack_send(ham_tiles, ham_send, ham_recv, pack_ref, 0)
    gather_start(full_ham, 0)

    loads[1].wait()
    for band in range(bands):
        lanes = slice(band * TW, (band + 1) * TW)
        value = jnp.where(mask_of(band), eta_ref[:, lanes], 0.0)
        eta_tiles[band * groups : (band + 1) * groups] = value.reshape(groups, TR, TW)
        high, low = split(value * pp_ref[:, lanes])
        lad_hi[:, lanes] = high
        lad_lo[:, lanes] = low

    wait_sent(ham_send, ham_recv, 0)
    pack_send(eta_tiles, eta_send, eta_recv, pack_ref, 1)

    def unpack(recv):
        @pl.loop(0, groups * bands // 16)
        def _(part):
            for inner in range(16):
                place = part * 16 + inner
                mixed[place] = recv[take_ref[place]]

    def band_tiles(band):
        return mixed[band * groups : (band + 1) * groups].reshape(rows, TW)

    loads[2].wait()
    for band in range(bands):
        square = split(coup_ref[band])
        squares[band] = dot3(square, square, ROW_DIMS)

    wait_arrived(ham_send, ham_recv, 0)
    unpack(ham_recv)
    for band in range(bands):
        total[:, band * TW : (band + 1) * TW] = dot3(
            split(band_tiles(band)), split(squares[band])
        )
    for part in range(rows // TW):
        band = row * (rows // TW) + part
        factors = ph_ref[:, pl.ds(pl.multiple_of(band * TW, TW), TW)]
        spot = slice(part * TW, (part + 1) * TW)
        full_ph[row, spot] = dot3(split(coup_ref[band] * factors), split(total[spot]))
    gather_start(full_ph, 1)
    gather_forward(full_ham, 0)
    gather_forward(full_ph, 1)

    gather_finish(full_ph, 1)
    for block in range(rgroups):
        high, low = split(full_ph[block])
        ph_hi[block] = high
        ph_lo[block] = low

    wait_arrived(eta_send, eta_recv, 1)
    unpack(eta_recv)
    for band in range(bands):
        lanes = slice(band * TW, (band + 1) * TW)
        high, low = split(band_tiles(band))
        left_hi[:, lanes] = high
        left_lo[:, lanes] = low

    def multiply(high_ref, low_ref, right, write):
        @pl.loop(0, cols // 256)
        def _(part):
            lanes = pl.ds(pl.multiple_of(part * 256, 256), 256)
            result = None
            for block in range(rgroups):
                depth = slice(block * rows, (block + 1) * rows)
                term = dot3((high_ref[:, depth], low_ref[:, depth]), right(block, lanes))
                result = term if result is None else result + term
            write(part, lanes, result)

    def write_tiles(part, lanes, result):
        for inner in range(256 // TW):
            value = result[:, inner * TW : (inner + 1) * TW].reshape(groups, TR, TW)
            band = part * (256 // TW) + inner
            mixed[pl.ds(band * groups, groups)] = value

    def write_rows(part, lanes, result):
        total[:, lanes] = result

    multiply(
        left_hi,
        left_lo,
        lambda block, lanes: (ph_hi[block, :, lanes], ph_lo[block, :, lanes]),
        write_tiles,
    )
    pack_send(mixed, back_send, back_recv, back_pack_ref, 2)

    gather_finish(full_ham, 0)
    multiply(
        lad_hi, lad_lo, lambda block, lanes: split(full_ham[block, :, lanes]), write_rows
    )
    wait_sent(eta_send, eta_recv, 1)
    gather_drain(full_ham, 0)
    gather_drain(full_ph, 1)

    wait_arrived(back_send, back_recv, 2)

    @pl.loop(0, groups)
    def _(group):
        spot = pl.ds(pl.multiple_of(group * TR, TR), TR)
        for band in range(bands):
            lanes = slice(band * TW, (band + 1) * TW)
            total[spot, lanes] += back_recv[back_take_ref[group * bands + band]]

    def turn_copy(target, source):
        return pltpu.make_async_remote_copy(
            src_ref=turned_send.at[target],
            dst_ref=turned_recv.at[source],
            send_sem=turn_send.at[target],
            recv_sem=turn_recv.at[source],
            device_id=(me, target),
            device_id_type=MESH,
        )

    def block_of(target):
        return total[:, pl.ds(pl.multiple_of(target * rows, rows), rows)]

    for target in (far, diagonal_peer, near):
        turned_send[target] = block_of(target).T
        turn_copy(target, row).start()

    own = block_of(row)
    turned_recv[row] = own.T
    eye_rows = lax.broadcasted_iota(jnp.int32, (rows, rows), 0)
    eye_cols = lax.broadcasted_iota(jnp.int32, (rows, rows), 1)
    diagonal = jnp.sum(jnp.where(eye_rows == eye_cols, own, 0.0), axis=0, keepdims=True)
    alive = row * rows + lax.broadcasted_iota(jnp.int32, (1, rows), 1) < size
    terms = jnp.where(alive, (diagonal + diagonal) * weight_ref[0], 0.0)
    orbit_ids = lax.broadcasted_iota(jnp.int32, (OPAD, rows), 0)
    table = (orbit_ids == orbit_ref[...]).astype(F32)
    row_sums[row] = lax.dot_general(
        jnp.broadcast_to(terms, (TR, rows)),
        table,
        ROW_DIMS,
        precision=lax.Precision.HIGHEST,
        preferred_element_type=F32,
    )

    def rsum_copy(target, source):
        return pltpu.make_async_remote_copy(
            src_ref=row_sums.at[row],
            dst_ref=row_sums.at[source],
            send_sem=rsum_send.at[target],
            recv_sem=rsum_recv.at[source],
            device_id=(me, target),
            device_id_type=MESH,
        )

    for target in (far, diagonal_peer, near):
        rsum_copy(target, row).start()
    for target in (far, diagonal_peer, near):
        rsum_copy(target, target).wait_recv()
    partial_value = row_sums[0]
    for block in range(1, rgroups):
        partial_value = partial_value + row_sums[block]
    chan_sums[me] = partial_value

    def csum_copy(target, source):
        return pltpu.make_async_remote_copy(
            src_ref=chan_sums.at[me],
            dst_ref=chan_sums.at[source],
            send_sem=csum_send.at[target],
            recv_sem=csum_recv.at[source],
            device_id=(target, row),
            device_id_type=MESH,
        )

    @pl.loop(1, n)
    def _(step):
        csum_copy(chan_peer(step), me).start()

    for target in (near, far, diagonal_peer):
        turn_copy(target, target).wait_recv()
    for block in range(rgroups):
        for part in range(rows // TW):
            band = block * (rows // TW) + part
            lanes = slice(band * TW, (band + 1) * TW)
            value = total[:, lanes] + turned_recv[block, :, part * TW : (part + 1) * TW]
            comm_ref[:, lanes] = jnp.where(mask_of(band), value, 0.0)

    @pl.loop(1, n)
    def _(step):
        peer = chan_peer(step)
        csum_copy(peer, peer).wait_recv()

    sums = lax.fori_loop(
        0, n, lambda i, acc: acc + chan_sums[i], jnp.zeros((TR, OPAD), F32)
    )
    onebody_ref[...] = sums[:1, :NORB] * math.sqrt(NORB / (n * cols))

    wait_sent(back_send, back_recv, 2)
    for target in (far, diagonal_peer, near):
        turn_copy(target, row).wait_send()
        rsum_copy(target, row).wait_send()

    @pl.loop(1, n)
    def _(step):
        csum_copy(chan_peer(step), me).wait_send()


def per_device(
    eta_pp,
    ham_pp,
    block_size,
    pp_occupancy,
    ph_occupancy,
    coupling,
    channel_weight,
    orbit_of,
    tile_target,
    tile_source,
):
    rows, cols = eta_pp.shape[1:]
    n = lax.axis_size("chan")
    rgroups = lax.axis_size("row")
    bands, groups = cols // TW, rows // TR
    count = bands * groups
    cap = max(2, 3 * count // (2 * n))
    slots = cap * n

    labels = jnp.stack([tile_target[0, 0], tile_source[0, 0]])
    slot_of = labels * cap + group_rank(labels)
    position = jnp.arange(count, dtype=jnp.int32)
    by_band = position % bands * groups + position // bands
    matches = slot_of[:, None, :] == jnp.arange(slots, dtype=jnp.int32)[None, :, None]
    pack = jnp.sum(jnp.where(matches, by_band, 0), axis=-1)
    take = slot_of[1].reshape(groups, bands).T.reshape(count)

    vmem = pl.BlockSpec(memory_space=pltpu.VMEM)
    hbm = pl.BlockSpec(memory_space=pl.ANY)
    smem = pl.BlockSpec(memory_space=pltpu.SMEM)
    dma = pltpu.SemaphoreType.DMA
    tile_buf = pltpu.VMEM((count, TR, TW), F32)
    slot_buf = pltpu.VMEM((slots, TR, TW), F32)
    full_buf = pltpu.VMEM((rgroups, rows, cols), F32)
    half_buf = pltpu.VMEM((rows, cols), BF16)
    comm, onebody = pl.pallas_call(
        functools.partial(kernel, n, cap),
        out_shape=(
            jax.ShapeDtypeStruct((rows, cols), F32),
            jax.ShapeDtypeStruct((1, NORB), F32),
        ),
        in_specs=[hbm, hbm, smem, vmem, vmem, hbm, smem, vmem, smem, smem, smem, smem],
        out_specs=(vmem, vmem),
        scratch_shapes=[
            pltpu.VMEM((rows, cols), F32),
            pltpu.VMEM((rows, cols), F32),
            pltpu.VMEM((bands, TW, TW), F32),
            pltpu.VMEM((bands, TW, TW), F32),
            pltpu.VMEM((rgroups, rows, cols), BF16),
            pltpu.VMEM((rgroups, rows, cols), BF16),
            tile_buf,
            tile_buf,
            slot_buf,
            slot_buf,
            slot_buf,
            slot_buf,
            full_buf,
            full_buf,
            tile_buf,
            half_buf,
            half_buf,
            half_buf,
            half_buf,
            pltpu.VMEM((rows, cols), F32),
            slot_buf,
            slot_buf,
            pltpu.VMEM((rgroups, rows, rows), F32),
            pltpu.VMEM((rgroups, rows, rows), F32),
            pltpu.VMEM((rgroups, TR, OPAD), F32),
            pltpu.VMEM((n, TR, OPAD), F32),
            dma((3,)),
            dma((3, n)),
            dma((3, n)),
            dma((2, 3)),
            dma((2, 3)),
            dma((rgroups,)),
            dma((rgroups,)),
            dma((rgroups,)),
            dma((rgroups,)),
            dma((n,)),
            dma((n,)),
        ],
        compiler_params=pltpu.CompilerParams(
            collective_id=0, has_side_effects=True, vmem_limit_bytes=56 * 1024 * 1024
        ),
    )(
        eta_pp[0],
        ham_pp[0],
        block_size,
        pp_occupancy,
        ph_occupancy,
        coupling[0],
        channel_weight,
        orbit_of,
        pack[0],
        take,
        pack[1],
        slot_of[0],
    )
    return comm[None], onebody.reshape(NORB)


def solution(mesh):
    return jax.shard_map(
        per_device,
        mesh=mesh,
        in_specs=(
            P("chan", "row", None),
            P("chan", "row", None),
            P("chan"),
            P("chan", None),
            P("chan", None),
            P("chan", None, None, None),
            P("chan"),
            P("chan", "row"),
            P("chan", "row", None),
            P("chan", "row", None),
        ),
        out_specs=(P("chan", "row", None), P()),
        check_vma=False,
    )
```

```python
import functools
import math

import jax
import jax.numpy as jnp
from jax import lax
from jax.experimental import pallas as pl
from jax.experimental.pallas import tpu as pltpu
from jax.sharding import PartitionSpec as P

TW = 128
TR = 8
NORB = 240
OPAD = 256
MESH = pl.DeviceIdType.MESH
F32 = jnp.float32
BF16 = jnp.bfloat16
ROW_DIMS = (((1,), (1,)), ((), ()))
COL_DIMS = (((1,), (0,)), ((), ()))


def group_rank(labels):
    length = labels.shape[-1]
    position = jnp.arange(length, dtype=jnp.int32)
    same_label = labels[:, :, None] == labels[:, None, :]
    before = position[None, :] < position[:, None]
    return jnp.sum((same_label & before).astype(jnp.int32), axis=-1)


def split(value):
    high = value.astype(BF16)
    return high, (value - high.astype(F32)).astype(BF16)


def dot3(left, right, dims=COL_DIMS):
    mul = functools.partial(lax.dot_general, dimension_numbers=dims, preferred_element_type=F32)
    return mul(left[0], right[0]) + (mul(left[0], right[1]) + mul(left[1], right[0]))


def kernel(
    n,
    cap,
    eta_hbm,
    ham_hbm,
    size_ref,
    pp_ref,
    ph_ref,
    coup_hbm,
    weight_ref,
    orbit_ref,
    pack_ref,
    take_ref,
    back_pack_ref,
    back_take_ref,
    comm_ref,
    onebody_ref,
    eta_ref,
    ham_ref,
    coup_ref,
    squares,
    ph_hi,
    ph_lo,
    ham_tiles,
    eta_tiles,
    ham_send,
    eta_send,
    ham_recv,
    eta_recv,
    full_ham,
    full_ph,
    mixed,
    left_hi,
    left_lo,
    lad_hi,
    lad_lo,
    total,
    back_send,
    back_recv,
    turned_send,
    turned_recv,
    row_sums,
    chan_sums,
    load_sem,
    a2a_send,
    a2a_recv,
    gather_send,
    gather_recv,
    turn_send,
    turn_recv,
    rsum_send,
    rsum_recv,
    csum_send,
    csum_recv,
):
    me = lax.axis_index("chan")
    row = lax.axis_index("row")
    rows, cols = eta_ref.shape
    rgroups = cols // rows
    bands = cols // TW
    groups = rows // TR
    near = row + 1 - 2 * lax.rem(row, 2)
    far = lax.rem(row + 2, rgroups)
    diagonal_peer = lax.rem(near + 2, rgroups)
    half = n // 2

    def chan_peer(step):
        away = step // 2
        sign = 2 * lax.rem(step, 2) - 1
        return lax.rem(me + half + sign * away + n, n)

    loads = [
        pltpu.make_async_copy(source, target, load_sem.at[place])
        for place, (source, target) in enumerate(
            ((ham_hbm, ham_ref), (eta_hbm, eta_ref), (coup_hbm, coup_ref))
        )
    ]
    for load in loads:
        load.start()

    barrier = pltpu.get_barrier_semaphore()

    @pl.loop(1, n)
    def _(step):
        pl.semaphore_signal(
            barrier, inc=1, device_id=(chan_peer(step), row), device_id_type=MESH
        )

    for other in range(1, rgroups):
        pl.semaphore_signal(
            barrier,
            inc=1,
            device_id=(me, lax.rem(row + other, rgroups)),
            device_id_type=MESH,
        )

    size = size_ref[0]
    row_ids = row * rows + lax.broadcasted_iota(jnp.int32, (rows, TW), 0)
    lane_ids = lax.broadcasted_iota(jnp.int32, (rows, TW), 1)

    def mask_of(band):
        return (row_ids < size) & (lane_ids + band * TW < size)

    loads[0].wait()
    for band in range(bands):
        lanes = slice(band * TW, (band + 1) * TW)
        value = jnp.where(mask_of(band), ham_ref[:, lanes], 0.0)
        full_ham[row, :, lanes] = value
        ham_tiles[band * groups : (band + 1) * groups] = value.reshape(groups, TR, TW)

    pl.semaphore_wait(barrier, n - 1 + rgroups - 1)

    chunks = 4
    chunk_rows = rows // chunks

    def gather_copy(buf, phase, kind, slot, target, chunk):
        place = buf.at[slot, pl.ds(chunk * chunk_rows, chunk_rows)]
        return pltpu.make_async_remote_copy(
            src_ref=place,
            dst_ref=place,
            send_sem=gather_send.at[phase, kind, chunk],
            recv_sem=gather_recv.at[phase, kind, chunk],
            device_id=(me, target),
            device_id_type=MESH,
        )

    def gather_start(buf, phase):
        for chunk in range(chunks):
            gather_copy(buf, phase, 0, row, far, chunk).start()
        for chunk in range(chunks):
            gather_copy(buf, phase, 1, row, near, chunk).start()

    def gather_forward(buf, phase):
        for chunk in range(chunks):
            gather_copy(buf, phase, 0, far, far, chunk).wait_recv()
            gather_copy(buf, phase, 2, far, near, chunk).start()

    def gather_finish(buf, phase):
        for chunk in range(chunks):
            gather_copy(buf, phase, 1, near, near, chunk).wait_recv()
            gather_copy(buf, phase, 2, diagonal_peer, near, chunk).wait_recv()

    def gather_drain(buf, phase):
        for chunk in range(chunks):
            gather_copy(buf, phase, 0, row, far, chunk).wait_send()
            gather_copy(buf, phase, 1, row, near, chunk).wait_send()
            gather_copy(buf, phase, 2, far, near, chunk).wait_send()

    unit = next(u for u in (16, 12, 8, 6, 4, 3, 2, 1) if cap % u == 0)

    def pack_one(tiles, out, table, peer, base):
        @pl.loop(0, cap // unit)
        def _(part):
            for inner in range(unit):
                place = part * unit + inner
                out[base + place] = tiles[table[peer * cap + place]]

    def send_copy(send, recv, phase, peer, source):
        return pltpu.make_async_remote_copy(
            src_ref=send.at[pl.ds(peer * cap, cap)],
            dst_ref=recv.at[pl.ds(source * cap, cap)],
            send_sem=a2a_send.at[phase, peer],
            recv_sem=a2a_recv.at[phase, source],
            device_id=(peer, row),
            device_id_type=MESH,
        )

    def pack_send(tiles, send, recv, table, phase):
        @pl.loop(1, n)
        def _(step):
            peer = chan_peer(step)
            pack_one(tiles, send, table, peer, peer * cap)
            send_copy(send, recv, phase, peer, me).start()

        pack_one(tiles, recv, table, me, me * cap)

    def wait_sent(send, recv, phase):
        @pl.loop(1, n)
        def _(step):
            send_copy(send, recv, phase, chan_peer(step), me).wait_send()

    def wait_arrived(send, recv, phase):
        @pl.loop(1, n)
        def _(step):
            peer = chan_peer(step)
            send_copy(send, recv, phase, peer, peer).wait_recv()

    pack_send(ham_tiles, ham_send, ham_recv, pack_ref, 0)
    gather_start(full_ham, 0)

    loads[1].wait()
    for band in range(bands):
        lanes = slice(band * TW, (band + 1) * TW)
        value = jnp.where(mask_of(band), eta_ref[:, lanes], 0.0)
        eta_tiles[band * groups : (band + 1) * groups] = value.reshape(groups, TR, TW)
        high, low = split(value * pp_ref[:, lanes])
        lad_hi[:, lanes] = high
        lad_lo[:, lanes] = low

    wait_sent(ham_send, ham_recv, 0)
    pack_send(eta_tiles, eta_send, eta_recv, pack_ref, 1)

    def unpack(recv):
        @pl.loop(0, groups * bands // 16)
        def _(part):
            for inner in range(16):
                place = part * 16 + inner
                mixed[place] = recv[take_ref[place]]

    def band_tiles(band):
        return mixed[band * groups : (band + 1) * groups].reshape(rows, TW)

    loads[2].wait()
    for band in range(bands):
        square = split(coup_ref[band])
        squares[band] = dot3(square, square, ROW_DIMS)

    gather_forward(full_ham, 0)
    wait_arrived(ham_send, ham_recv, 0)
    unpack(ham_recv)
    for band in range(bands):
        total[:, band * TW : (band + 1) * TW] = dot3(
            split(band_tiles(band)), split(squares[band])
        )
    for part in range(rows // TW):
        band = row * (rows // TW) + part
        factors = ph_ref[:, pl.ds(pl.multiple_of(band * TW, TW), TW)]
        spot = slice(part * TW, (part + 1) * TW)
        full_ph[row, spot] = dot3(split(coup_ref[band] * factors), split(total[spot]))
    gather_start(full_ph, 1)
    gather_forward(full_ph, 1)

    gather_finish(full_ph, 1)
    for block in range(rgroups):
        high, low = split(full_ph[block])
        ph_hi[block] = high
        ph_lo[block] = low

    wait_arrived(eta_send, eta_recv, 1)
    unpack(eta_recv)
    for band in range(bands):
        lanes = slice(band * TW, (band + 1) * TW)
        high, low = split(band_tiles(band))
        left_hi[:, lanes] = high
        left_lo[:, lanes] = low

    def multiply(high_ref, low_ref, right, write):
        @pl.loop(0, cols // 256)
        def _(part):
            lanes = pl.ds(pl.multiple_of(part * 256, 256), 256)
            result = None
            for block in range(rgroups):
                depth = slice(block * rows, (block + 1) * rows)
                term = dot3((high_ref[:, depth], low_ref[:, depth]), right(block, lanes))
                result = term if result is None else result + term
            write(part, lanes, result)

    def write_tiles(part, lanes, result):
        for inner in range(256 // TW):
            value = result[:, inner * TW : (inner + 1) * TW].reshape(groups, TR, TW)
            band = part * (256 // TW) + inner
            mixed[pl.ds(band * groups, groups)] = value

    def write_rows(part, lanes, result):
        total[:, lanes] = result

    multiply(
        left_hi,
        left_lo,
        lambda block, lanes: (ph_hi[block, :, lanes], ph_lo[block, :, lanes]),
        write_tiles,
    )
    pack_send(mixed, back_send, back_recv, back_pack_ref, 2)

    gather_finish(full_ham, 0)
    multiply(
        lad_hi, lad_lo, lambda block, lanes: split(full_ham[block, :, lanes]), write_rows
    )
    wait_sent(eta_send, eta_recv, 1)
    gather_drain(full_ham, 0)
    gather_drain(full_ph, 1)

    wait_arrived(back_send, back_recv, 2)

    block_bands = rows // TW

    def add_back(target):
        @pl.loop(0, groups // 4)
        def _(part):
            for inner in range(4):
                group = part * 4 + inner
                spot = pl.ds(pl.multiple_of(group * TR, TR), TR)
                for index in range(block_bands):
                    band = target * block_bands + index
                    lanes = pl.ds(pl.multiple_of(band * TW, TW), TW)
                    total[spot, lanes] += back_recv[back_take_ref[group * bands + band]]

    def turn_copy(target, source):
        return pltpu.make_async_remote_copy(
            src_ref=turned_send.at[target],
            dst_ref=turned_recv.at[source],
            send_sem=turn_send.at[target],
            recv_sem=turn_recv.at[source],
            device_id=(me, target),
            device_id_type=MESH,
        )

    def block_of(target):
        return total[:, pl.ds(pl.multiple_of(target * rows, rows), rows)]

    add_back(row)
    own = block_of(row)
    turned_recv[row] = own.T
    eye_rows = lax.broadcasted_iota(jnp.int32, (rows, rows), 0)
    eye_cols = lax.broadcasted_iota(jnp.int32, (rows, rows), 1)
    diagonal = jnp.sum(jnp.where(eye_rows == eye_cols, own, 0.0), axis=0, keepdims=True)
    alive = row * rows + lax.broadcasted_iota(jnp.int32, (1, rows), 1) < size
    terms = jnp.where(alive, (diagonal + diagonal) * weight_ref[0], 0.0)
    orbit_ids = lax.broadcasted_iota(jnp.int32, (OPAD, rows), 0)
    table = (orbit_ids == orbit_ref[...]).astype(F32)
    row_sums[row] = lax.dot_general(
        jnp.broadcast_to(terms, (TR, rows)),
        table,
        ROW_DIMS,
        precision=lax.Precision.HIGHEST,
        preferred_element_type=F32,
    )

    def rsum_copy(target, source):
        return pltpu.make_async_remote_copy(
            src_ref=row_sums.at[row],
            dst_ref=row_sums.at[source],
            send_sem=rsum_send.at[target],
            recv_sem=rsum_recv.at[source],
            device_id=(me, target),
            device_id_type=MESH,
        )

    for target in (far, diagonal_peer, near):
        rsum_copy(target, row).start()
    for target in (far, diagonal_peer, near):
        add_back(target)
        turned_send[target] = block_of(target).T
        turn_copy(target, row).start()

    for target in (far, diagonal_peer, near):
        rsum_copy(target, target).wait_recv()
    partial_value = row_sums[0]
    for block in range(1, rgroups):
        partial_value = partial_value + row_sums[block]
    chan_sums[me] = partial_value

    def csum_copy(target, source):
        return pltpu.make_async_remote_copy(
            src_ref=chan_sums.at[me],
            dst_ref=chan_sums.at[source],
            send_sem=csum_send.at[target],
            recv_sem=csum_recv.at[source],
            device_id=(target, row),
            device_id_type=MESH,
        )

    @pl.loop(1, n)
    def _(step):
        csum_copy(chan_peer(step), me).start()

    for target in (row, near, far, diagonal_peer):
        if target is not row:
            turn_copy(target, target).wait_recv()
        for part in range(block_bands):
            band = target * block_bands + part
            lanes = pl.ds(pl.multiple_of(band * TW, TW), TW)
            value = total[:, lanes] + turned_recv[target, :, part * TW : (part + 1) * TW]
            comm_ref[:, lanes] = jnp.where(mask_of(band), value, 0.0)

    @pl.loop(1, n)
    def _(step):
        peer = chan_peer(step)
        csum_copy(peer, peer).wait_recv()

    sums = lax.fori_loop(
        0, n, lambda i, acc: acc + chan_sums[i], jnp.zeros((TR, OPAD), F32)
    )
    onebody_ref[...] = sums[:1, :NORB] * math.sqrt(NORB / (n * cols))

    wait_sent(back_send, back_recv, 2)
    for target in (far, diagonal_peer, near):
        turn_copy(target, row).wait_send()
        rsum_copy(target, row).wait_send()

    @pl.loop(1, n)
    def _(step):
        csum_copy(chan_peer(step), me).wait_send()


def per_device(
    eta_pp,
    ham_pp,
    block_size,
    pp_occupancy,
    ph_occupancy,
    coupling,
    channel_weight,
    orbit_of,
    tile_target,
    tile_source,
):
    rows, cols = eta_pp.shape[1:]
    n = lax.axis_size("chan")
    rgroups = lax.axis_size("row")
    bands, groups = cols // TW, rows // TR
    count = bands * groups
    cap = max(2, 3 * count // (2 * n))
    slots = cap * n

    labels = jnp.stack([tile_target[0, 0], tile_source[0, 0]])
    slot_of = labels * cap + group_rank(labels)
    position = jnp.arange(count, dtype=jnp.int32)
    by_band = position % bands * groups + position // bands
    matches = slot_of[:, None, :] == jnp.arange(slots, dtype=jnp.int32)[None, :, None]
    pack = jnp.sum(jnp.where(matches, by_band, 0), axis=-1)
    take = slot_of[1].reshape(groups, bands).T.reshape(count)

    vmem = pl.BlockSpec(memory_space=pltpu.VMEM)
    hbm = pl.BlockSpec(memory_space=pl.ANY)
    smem = pl.BlockSpec(memory_space=pltpu.SMEM)
    dma = pltpu.SemaphoreType.DMA
    tile_buf = pltpu.VMEM((count, TR, TW), F32)
    slot_buf = pltpu.VMEM((slots, TR, TW), F32)
    full_buf = pltpu.VMEM((rgroups, rows, cols), F32)
    half_buf = pltpu.VMEM((rows, cols), BF16)
    comm, onebody = pl.pallas_call(
        functools.partial(kernel, n, cap),
        out_shape=(
            jax.ShapeDtypeStruct((rows, cols), F32),
            jax.ShapeDtypeStruct((1, NORB), F32),
        ),
        in_specs=[hbm, hbm, smem, vmem, vmem, hbm, smem, vmem, smem, smem, smem, smem],
        out_specs=(vmem, vmem),
        scratch_shapes=[
            pltpu.VMEM((rows, cols), F32),
            pltpu.VMEM((rows, cols), F32),
            pltpu.VMEM((bands, TW, TW), F32),
            pltpu.VMEM((bands, TW, TW), F32),
            pltpu.VMEM((rgroups, rows, cols), BF16),
            pltpu.VMEM((rgroups, rows, cols), BF16),
            tile_buf,
            tile_buf,
            slot_buf,
            slot_buf,
            slot_buf,
            slot_buf,
            full_buf,
            full_buf,
            tile_buf,
            half_buf,
            half_buf,
            half_buf,
            half_buf,
            pltpu.VMEM((rows, cols), F32),
            slot_buf,
            slot_buf,
            pltpu.VMEM((rgroups, rows, rows), F32),
            pltpu.VMEM((rgroups, rows, rows), F32),
            pltpu.VMEM((rgroups, TR, OPAD), F32),
            pltpu.VMEM((n, TR, OPAD), F32),
            dma((3,)),
            dma((3, n)),
            dma((3, n)),
            dma((2, 3, 4)),
            dma((2, 3, 4)),
            dma((rgroups,)),
            dma((rgroups,)),
            dma((rgroups,)),
            dma((rgroups,)),
            dma((n,)),
            dma((n,)),
        ],
        compiler_params=pltpu.CompilerParams(
            collective_id=0, has_side_effects=True, vmem_limit_bytes=42 * 1024 * 1024
        ),
    )(
        eta_pp[0],
        ham_pp[0],
        block_size,
        pp_occupancy,
        ph_occupancy,
        coupling[0],
        channel_weight,
        orbit_of,
        pack[0],
        take,
        pack[1],
        slot_of[0],
    )
    return comm[None], onebody.reshape(NORB)


def solution(mesh):
    return jax.shard_map(
        per_device,
        mesh=mesh,
        in_specs=(
            P("chan", "row", None),
            P("chan", "row", None),
            P("chan"),
            P("chan", None),
            P("chan", None),
            P("chan", None, None, None),
            P("chan"),
            P("chan", "row"),
            P("chan", "row", None),
            P("chan", "row", None),
        ),
        out_specs=(P("chan", "row", None), P()),
        check_vma=False,
    )
```
